32 devices in a mesh: rows: 4 (over x, core), freq: 8 (over z, y).
Axes of the slice: x: 2, y: 2, z: 4, core: 2. Of those that a mesh axis runs over, the one named last changes fastest.
Arguments:
- measure_weight_spectra: bfloat16 [3072, 2048, 128], P('rows', 'freq'), may hold values from -0.19921875 to 0.19921875
- spectral_power: float32 [2048, 64], P('freq'), may hold values from 0.125 to 8, as said below
- pair_list: int32 [64, 2], P('rows'), may hold values from 0 to 23, as said below
Outputs:
- noise_covariance_tiles: float32 [64, 128, 128], P(('rows', 'freq'))
The draws below stay inside these ranges and needn't reach their ends.
Inputs may be any that keep to these rules, and one draw needn't show every extreme that they name: `spectral_power`: every value is 0.125, 0.5, 2 or 8. `pair_list`: pairs 16 g to 16 (g + 1) - 1 form row group g: their row block lies in g * 6 to (g + 1) * 6 - 1, and their column block is the row block plus a nonzero offset of -4 to 4, taken modulo 24 (the line of measurements closes on itself). Each group holds a pair with offset -4 and one with offset 4. Pairs may repeat.
All inputs are finite; a program needn't handle non-finite values.
Results may differ from the reference program's by a relative error of at most 0.0003.
Values may be sent and summed in bfloat16 or wider, within the bound.
A program may use at most 448 MiB of HBM per device.

```python
import jax
import jax.numpy as jnp
from jax import lax

FREQUENCY_COUNT = 2048
WAVENUMBER_COUNT = 64
TILE = 128
BLK_DEV = 6
REACH = 4
PAIRS_GRP = 16
PAIRS = 64
BLOCKS = 24
MEASURE_COUNT = 3072


def draw_spectral_power(key, part):
    key = jax.random.fold_in(key, 11)
    level = jax.random.randint(key, (FREQUENCY_COUNT, WAVENUMBER_COUNT), 0, 4, dtype=jnp.int32)
    table = jnp.array([0.125, 0.5, 2.0, 8.0], dtype=jnp.float32)
    return jnp.take(table, level).astype(jnp.float32)


def draw_pair_list(key, part):
    index_all = jnp.arange(PAIRS, dtype=jnp.int32)
    row_group = index_all // PAIRS_GRP
    slot_number = index_all % PAIRS_GRP
    first_key, second_key = jax.random.split(jax.random.fold_in(key, 7))
    local_block = jax.random.randint(first_key, (PAIRS,), 0, BLK_DEV, dtype=jnp.int32)
    offsets = jax.random.randint(second_key, (PAIRS,), -REACH, REACH, dtype=jnp.int32)
    offsets = jnp.where(offsets >= 0, offsets + 1, offsets)
    offsets = jnp.where(slot_number == 1, -REACH, jnp.where(slot_number == 2, REACH, offsets))
    local_block = jnp.where(index_all == 0, 0, jnp.where(index_all == PAIRS - 1, BLK_DEV - 1, local_block))
    row_block = row_group * BLK_DEV + local_block
    col_block = jnp.remainder(row_block + offsets, BLOCKS)
    return jnp.stack([row_block, col_block], axis=1).astype(jnp.int32)


def level_of(own_key, dims, cuts, smallest, high):
    level, own = 1.0, jax.random.fold_in(own_key, 6)
    for dim, shards_of in cuts:
        steps = jnp.exp(jax.random.uniform(jax.random.fold_in(own, dim), (shards_of,), jnp.float32, smallest / len(cuts), high / len(cuts)))
        level = level * jnp.repeat(steps, dims[dim] // shards_of).reshape([-1 if axis == dim else 1 for axis in range(len(dims))])
    return level


def normal_values(stream_key, extent, width, bound, shards=(), kind=jnp.bfloat16):
    factor_of = level_of(stream_key, extent, shards, -0.22, 0.18) if shards else 1.0
    values = jax.random.normal(stream_key, extent, jnp.float32) * width * factor_of
    return jnp.minimum(jnp.maximum(values, -bound), bound).astype(kind)


def setup_inputs(seed: int = 0) -> dict:
    arg_keys = jax.random.split(jax.random.key(seed), 4)
    return {
        "measure_weight_spectra": normal_values(arg_keys[0], (MEASURE_COUNT, FREQUENCY_COUNT, 2 * WAVENUMBER_COUNT), 0.025, 0.19921875, ((0, 4), (1, 8))),
        "spectral_power": draw_spectral_power(jax.random.fold_in(arg_keys[3], 71), 0),
        "pair_list": draw_pair_list(jax.random.fold_in(arg_keys[3], 71), 0),
    }


def reference(measure_weight_spectra, spectral_power, pair_list):
    blocks_all = measure_weight_spectra.reshape(BLOCKS, TILE, FREQUENCY_COUNT * 2 * WAVENUMBER_COUNT)
    weighting = jnp.concatenate([spectral_power, spectral_power], axis=1).reshape(-1).astype(jnp.float32)

    def one_tile(pair_row):
        row_block = blocks_all[pair_row[0]].astype(jnp.float32)
        col_block = blocks_all[pair_row[1]].astype(jnp.float32)
        scaled = (row_block * weighting).astype(jnp.bfloat16)
        scaled = lax.optimization_barrier(scaled).astype(jnp.float32)
        return jnp.dot(scaled, col_block.T, precision=lax.Precision.HIGHEST)

    return lax.map(one_tile, pair_list)
```

```python
import functools

import jax
import jax.numpy as jnp
from jax import lax
from jax.experimental import pallas as pl
from jax.experimental.pallas import tpu as pltpu
from jax.sharding import PartitionSpec as P

TILE = 128
REACH = 4
STEP = 32
MESH = pl.DeviceIdType.MESH


def sum_kernel(peers, parts_ref, out_ref, landed, send_sem, recv_sem):
    me = lax.axis_index("freq")
    row = lax.axis_index("rows")
    own = out_ref.shape[0]

    barrier = pltpu.get_barrier_semaphore()

    def greet(step, carry):
        pl.semaphore_signal(barrier, inc=1, device_id=(row, lax.rem(me + step, peers)), device_id_type=MESH)
        return carry

    lax.fori_loop(1, peers, greet, 0)
    pl.semaphore_wait(barrier, peers - 1)

    def copy_to(step):
        peer = lax.rem(me + step, peers)
        return pltpu.make_async_remote_copy(
            src_ref=parts_ref.at[pl.ds(peer * own, own)],
            dst_ref=landed.at[step],
            send_sem=send_sem.at[step],
            recv_sem=recv_sem.at[step],
            device_id=(row, peer),
            device_id_type=MESH,
        )

    def send(step, carry):
        copy_to(step).start()
        return carry

    lax.fori_loop(1, peers, send, 0)
    out_ref[...] = parts_ref[pl.ds(me * own, own)]

    def receive(step, carry):
        copy_to(step).wait()
        out_ref[...] += landed[step]
        return carry

    lax.fori_loop(1, peers, receive, 0)


def summed_share(parts):
    peers = lax.axis_size("freq")
    own = parts.shape[0] // peers
    return pl.pallas_call(
        functools.partial(sum_kernel, peers),
        out_shape=jax.ShapeDtypeStruct((own, TILE, TILE), jnp.float32),
        in_specs=[pl.BlockSpec(memory_space=pltpu.VMEM)],
        out_specs=pl.BlockSpec(memory_space=pltpu.VMEM),
        scratch_shapes=[
            pltpu.VMEM((peers, own, TILE, TILE), jnp.float32),
            pltpu.SemaphoreType.DMA((peers,)),
            pltpu.SemaphoreType.DMA((peers,)),
        ],
        compiler_params=pltpu.CompilerParams(
            collective_id=0, has_side_effects=True, vmem_limit_bytes=40 * 1024 * 1024
        ),
    )(parts)


def gram(left, right):
    return lax.dot_general(left, right, (((1, 2), (1, 2)), ((), ())), preferred_element_type=jnp.float32)


def shards(measure_weight_spectra, spectral_power, pair_list):
    spectra = measure_weight_spectra
    rows_here, freq_here, lane_width = spectra.shape
    present_blocks = rows_here // TILE
    groups = lax.axis_size("rows")
    block_count = present_blocks * groups
    edge = REACH * TILE
    weighting = jnp.concatenate([spectral_power, spectral_power], axis=1)
    half = STEP // 2
    middle = freq_here - 2 * half
    sizes = [half] + [STEP] * (middle // STEP) + [half] * (middle % STEP // half) + [half]
    cuts = [(sum(sizes[:k]), size) for k, size in enumerate(sizes)]
    up = [(i, (i + 1) % groups) for i in range(groups)]
    down = [(j, i) for i, j in up]

    received, start = [], jnp.zeros((), jnp.int32)
    for k, (at, depth) in enumerate(cuts):
        if k >= 3:
            start, received[k - 3] = lax.optimization_barrier((start, received[k - 3]))
        part = lax.dynamic_slice(
            spectra, (rows_here - edge, start + at, 0), (edge, depth, lane_width)
        )
        start, part = lax.optimization_barrier((start, part))
        received.append(lax.ppermute(part, "rows", up))
        if k == 1:
            begin = start

    inner = jnp.zeros((rows_here, rows_here), jnp.float32)
    cross = jnp.zeros((edge, edge), jnp.float32)
    for k, (at, depth) in enumerate(cuts):
        raw = lax.dynamic_slice(spectra, (0, begin + at, 0), (rows_here, depth, lane_width))
        raw = lax.optimization_barrier(raw)
        scale = lax.slice_in_dim(weighting, at, at + depth, axis=0)
        scaled = (raw.astype(jnp.float32) * scale).astype(jnp.bfloat16)
        inner = inner + gram(scaled, raw)
        cross = cross + gram(scaled[:edge], received[k])
        begin, inner, cross = lax.optimization_barrier((begin, inner, cross))

    def tiles_of(matrix, transposed):
        side = matrix.shape[0] // TILE
        order = (2, 0, 3, 1) if transposed else (0, 2, 1, 3)
        return matrix.reshape(side, TILE, side, TILE).transpose(order).reshape(side * side, TILE, TILE)

    ahead = lax.ppermute(cross, "rows", down)
    table = jnp.concatenate([tiles_of(inner, False), tiles_of(cross, False), tiles_of(ahead, True)], axis=0)

    first = lax.axis_index("rows") * present_blocks
    row_at = pair_list[:, 0] - first
    offset = jnp.remainder(pair_list[:, 1] - pair_list[:, 0] + REACH, block_count) - REACH
    col_at = row_at + offset
    inner_at = row_at * present_blocks + col_at
    behind_at = present_blocks**2 + row_at * REACH + col_at + REACH
    ahead_at = present_blocks**2 + REACH**2 + (row_at - present_blocks + REACH) * REACH + col_at - present_blocks
    index = jnp.where(col_at < 0, behind_at, jnp.where(col_at >= present_blocks, ahead_at, inner_at))
    return summed_share(jnp.take(table, index, axis=0))


def solution(mesh):
    in_specs = (P("rows", "freq", None), P("freq", None), P("rows", None))
    out_specs = P(("rows", "freq"), None, None)
    return jax.shard_map(shards, mesh=mesh, in_specs=in_specs, out_specs=out_specs, check_vma=False)
```

```python
import functools

import jax
import jax.numpy as jnp
from jax import lax
from jax.experimental import pallas as pl
from jax.experimental.pallas import tpu as pltpu
from jax.sharding import PartitionSpec as P

TILE = 128
REACH = 4
STEP = 32
MESH = pl.DeviceIdType.MESH


def sum_kernel(peers, parts_ref, out_ref, landed, send_sem, recv_sem):
    me = lax.axis_index("freq")
    row = lax.axis_index("rows")
    own = out_ref.shape[0]

    barrier = pltpu.get_barrier_semaphore()

    def greet(step, carry):
        pl.semaphore_signal(barrier, inc=1, device_id=(row, lax.rem(me + step, peers)), device_id_type=MESH)
        return carry

    lax.fori_loop(1, peers, greet, 0)
    pl.semaphore_wait(barrier, peers - 1)

    def copy_to(step):
        peer = lax.rem(me + step, peers)
        return pltpu.make_async_remote_copy(
            src_ref=parts_ref.at[pl.ds(peer * own, own)],
            dst_ref=landed.at[step],
            send_sem=send_sem.at[step],
            recv_sem=recv_sem.at[step],
            device_id=(row, peer),
            device_id_type=MESH,
        )

    def send(step, carry):
        copy_to(step).start()
        return carry

    lax.fori_loop(1, peers, send, 0)
    out_ref[...] = parts_ref[pl.ds(me * own, own)]

    def receive(step, carry):
        copy_to(step).wait()
        out_ref[...] += landed[step]
        return carry

    lax.fori_loop(1, peers, receive, 0)


def summed_share(parts):
    peers = lax.axis_size("freq")
    own = parts.shape[0] // peers
    return pl.pallas_call(
        functools.partial(sum_kernel, peers),
        out_shape=jax.ShapeDtypeStruct((own, TILE, TILE), jnp.float32),
        in_specs=[pl.BlockSpec(memory_space=pltpu.VMEM)],
        out_specs=pl.BlockSpec(memory_space=pltpu.VMEM),
        scratch_shapes=[
            pltpu.VMEM((peers, own, TILE, TILE), jnp.float32),
            pltpu.SemaphoreType.DMA((peers,)),
            pltpu.SemaphoreType.DMA((peers,)),
        ],
        compiler_params=pltpu.CompilerParams(
            collective_id=0, has_side_effects=True, vmem_limit_bytes=40 * 1024 * 1024
        ),
    )(parts)


def gram(left, right):
    return lax.dot_general(left, right, (((1, 2), (1, 2)), ((), ())), preferred_element_type=jnp.float32)


def shards(measure_weight_spectra, spectral_power, pair_list):
    spectra = measure_weight_spectra
    rows_here, freq_here, lane_width = spectra.shape
    present_blocks = rows_here // TILE
    groups = lax.axis_size("rows")
    block_count = present_blocks * groups
    edge = REACH * TILE
    weighting = jnp.concatenate([spectral_power, spectral_power], axis=1)
    half = STEP // 2
    middle = freq_here - 2 * half
    sizes = [half] + [STEP] * (middle // STEP) + [half] * (middle % STEP // half) + [half]
    cuts = [(sum(sizes[:k]), size) for k, size in enumerate(sizes)]
    up = [(i, (i + 1) % groups) for i in range(groups)]
    down = [(j, i) for i, j in up]

    received, start = [], jnp.zeros((), jnp.int32)
    for k, (at, depth) in enumerate(cuts):
        if k >= 4:
            start, received[k - 4] = lax.optimization_barrier((start, received[k - 4]))
        part = lax.dynamic_slice(
            spectra, (rows_here - edge, start + at, 0), (edge, depth, lane_width)
        )
        start, part = lax.optimization_barrier((start, part))
        received.append(lax.ppermute(part, "rows", up))
        if k == 1:
            begin = start

    inner = jnp.zeros((rows_here, rows_here), jnp.float32)
    cross = jnp.zeros((edge, edge), jnp.float32)
    for k, (at, depth) in enumerate(cuts):
        raw = lax.dynamic_slice(spectra, (0, begin + at, 0), (rows_here, depth, lane_width))
        raw = lax.optimization_barrier(raw)
        scale = lax.slice_in_dim(weighting, at, at + depth, axis=0)
        scaled = (raw.astype(jnp.float32) * scale).astype(jnp.bfloat16)
        inner = inner + gram(scaled, raw)
        cross = cross + gram(scaled[:edge], received[k])
        begin, inner, cross = lax.optimization_barrier((begin, inner, cross))

    def tiles_of(matrix, transposed):
        side = matrix.shape[0] // TILE
        order = (2, 0, 3, 1) if transposed else (0, 2, 1, 3)
        return matrix.reshape(side, TILE, side, TILE).transpose(order).reshape(side * side, TILE, TILE)

    ahead = lax.ppermute(cross, "rows", down)
    table = jnp.concatenate([tiles_of(inner, False), tiles_of(cross, False), tiles_of(ahead, True)], axis=0)

    first = lax.axis_index("rows") * present_blocks
    row_at = pair_list[:, 0] - first
    offset = jnp.remainder(pair_list[:, 1] - pair_list[:, 0] + REACH, block_count) - REACH
    col_at = row_at + offset
    inner_at = row_at * present_blocks + col_at
    behind_at = present_blocks**2 + row_at * REACH + col_at + REACH
    ahead_at = present_blocks**2 + REACH**2 + (row_at - present_blocks + REACH) * REACH + col_at - present_blocks
    index = jnp.where(col_at < 0, behind_at, jnp.where(col_at >= present_blocks, ahead_at, inner_at))
    return summed_share(jnp.take(table, index, axis=0))


def solution(mesh):
    in_specs = (P("rows", "freq", None), P("freq", None), P("rows", None))
    out_specs = P(("rows", "freq"), None, None)
    return jax.shard_map(shards, mesh=mesh, in_specs=in_specs, out_specs=out_specs, check_vma=False)
```
